128 devices in a mesh: dp: 2 (over core), ctx: 16 (over y, z), tp: 4 (over x).
Axes of the slice: x: 4, y: 4, z: 4, core: 2. Of those that a mesh axis runs over, the one named last changes fastest.
Arguments:
- response: bfloat16 [32, 512, 4096], P(('dp', 'ctx'), None, 'tp'), parts along dimension 0, may hold values from -6 to 6
- owner: int32 [2], P('dp'), parts along dimension 0, may hold values from 0 to 15, as said below
- doc_lengths: int32 [32], P(('dp', 'ctx')), parts along dimension 0, may hold values from 512 to 2048, as said below
- doc_keys: bfloat16 [65536, 8, 128], P(('dp', 'ctx'), 'tp'), parts along dimension 0, may hold values from -2000 to 2000
- doc_values: bfloat16 [65536, 8, 128], P(('dp', 'ctx'), 'tp'), parts along dimension 0, may hold values from -6 to 6
- w_query: bfloat16 [4096, 4096], P(None, 'tp'), may hold values from -0.09375 to 0.09375
- w_key: bfloat16 [4096, 1024], P(None, 'tp'), may hold values from -0.375 to 0.375
- w_value: bfloat16 [4096, 1024], P(None, 'tp'), may hold values from -0.09375 to 0.09375
- w_out: bfloat16 [4096, 4096], P('tp'), may hold values from -0.09375 to 0.09375
Outputs:
- layer_out: bfloat16 [1024, 4096], P(('dp', 'ctx'), 'tp'), parts along dimension 0
The draws below stay inside these ranges and needn't reach their ends.
There are 2 independent parts, one for each index of `dp`. The reference program is written for one: setup_inputs(seed, part) draws one part's arguments, and reference() takes and returns one part's arrays. A program takes and returns all parts, laid end to end along the dimension named above; an argument that names none is the same for every part. Nothing has to cross between parts.
Inputs may be any that keep to these rules, and one draw needn't show every extreme that they name: The first part's owner lies in the lower half of ctx's indices; the second part's owner is the last index, 15. `doc_lengths`: some index of ctx has a full cache in every draw.
All inputs are finite; a program needn't handle non-finite values.
Results may differ from the reference program's by a relative error of at most 0.014.
The reference program's roundings to bfloat16 on the way (of `hidden_rows`, `queries`, `weights` and `attended`) count: a program that leaves them out, or rounds other values in their place, can miss the bound.
Values may be sent and summed in bfloat16 or wider, within the bound.
No kernel may reach another device: no remote copies, remote signals or barrier semaphores. Data moves between devices by JAX's collectives and lax.ppermute only.
A program may use at most 192 MiB of HBM per device.

```python
import jax
import jax.numpy as jnp
from jax import lax

D = 4096
HEADS = 32
KV_HEADS = 8
HEAD_DIM = 128
RESP = 512
S_DEV = 2048
DOC = 32768
N_CTX = 16


def draw_owner(key, part):
    key = jax.random.fold_in(key, 13)
    half = N_CTX // 2
    offset = jax.random.randint(key, (1,), 0, half)
    upper = jnp.full((1,), N_CTX - 1, jnp.int32)
    return jnp.where(part % 2 == 1, upper, offset).astype(jnp.int32)


def draw_doc_lengths(key, part):
    key = jax.random.fold_in(key, 12)
    filled = jax.random.randint(jax.random.fold_in(key, 1), (N_CTX,), S_DEV // 4, S_DEV + 1)
    chosen = jax.random.randint(jax.random.fold_in(key, 2), (), 0, N_CTX)
    return filled.at[chosen].set(S_DEV).astype(jnp.int32)


def draw_doc_keys(key, part):
    key = jax.random.fold_in(key, 11)
    shape = (N_CTX * S_DEV, KV_HEADS, HEAD_DIM)
    cached = 3.0 * jnp.clip(jax.random.normal(key, shape, jnp.float32), -6.0, 6.0)
    return cached.astype(jnp.bfloat16)


def levels(rng, dims, pieces, low, high):
    loudness = 1.0
    for axis_at, parts in pieces:
        draws = jax.random.uniform(jax.random.fold_in(jax.random.fold_in(rng, 6), axis_at), (parts,), jnp.float32, low / len(pieces), high / len(pieces))
        loudness = loudness * jnp.repeat(jnp.exp(draws), dims[axis_at] // parts).reshape((-1,) + (1,) * (len(dims) - 1 - axis_at))
    return loudness


def centred(rng, shape, width, bound, shards=(), dtype=jnp.bfloat16):
    array = width * jax.random.normal(rng, shape, jnp.float32)
    if shards:
        array = array * levels(rng, shape, shards, -0.22, 0.18)
    return jnp.clip(array, -bound, bound).astype(dtype)


def setup_inputs(seed: int = 0, part: int = 0) -> dict:
    splits = jax.random.split(jax.random.key(seed), 10)
    part_keys = jax.random.split(jax.random.fold_in(splits[9], part), 10)
    response = centred(part_keys[0], (N_CTX, RESP, D), 1.0, 6.0, ((0, 16), (2, 4)))
    owner = draw_owner(jax.random.fold_in(jax.random.fold_in(splits[9], part), 71), part)
    doc_lengths = draw_doc_lengths(jax.random.fold_in(jax.random.fold_in(splits[9], part), 71), part)
    doc_keys = draw_doc_keys(jax.random.fold_in(jax.random.fold_in(splits[9], part), 71), part)
    doc_values = centred(part_keys[4], (DOC, KV_HEADS, HEAD_DIM), 1.0, 6.0, ((0, 16), (1, 4)))
    w_query = centred(splits[5], (D, HEADS * HEAD_DIM), D ** -0.5, 0.09375, ((1, 4),))
    w_key = centred(splits[6], (D, KV_HEADS * HEAD_DIM), (D // 16) ** -0.5, 0.375, ((1, 4),))
    w_value = centred(splits[7], (D, KV_HEADS * HEAD_DIM), D ** -0.5, 0.09375, ((1, 4),))
    w_out = centred(splits[8], (HEADS * HEAD_DIM, D), (HEADS * HEAD_DIM) ** -0.5, 0.09375, ((0, 4),))
    return {"response": response, "owner": owner, "doc_lengths": doc_lengths, "doc_keys": doc_keys, "doc_values": doc_values, "w_query": w_query, "w_key": w_key, "w_value": w_value, "w_out": w_out}


def reference(response, owner, doc_lengths, doc_keys, doc_values, w_query, w_key, w_value, w_out):
    row_count = response.shape[1]
    hidden_rows = lax.dynamic_index_in_dim(response, owner[0].astype(jnp.int32), 0, keepdims=False)
    queries = jnp.dot(hidden_rows, w_query, preferred_element_type=jnp.float32).astype(jnp.bfloat16)
    self_keys = jnp.dot(hidden_rows, w_key, preferred_element_type=jnp.float32).astype(jnp.bfloat16)
    self_values = jnp.dot(hidden_rows, w_value, preferred_element_type=jnp.float32).astype(jnp.bfloat16)
    total = N_CTX * S_DEV
    position = jnp.arange(total)
    doc_visible = (position % S_DEV) < doc_lengths[position // S_DEV]
    causal = jnp.arange(row_count)[None, :] <= jnp.arange(row_count)[:, None]
    visible = jnp.concatenate([jnp.broadcast_to(doc_visible[None, :], (row_count, total)), causal], 1)
    group_size = HEADS // KV_HEADS
    query_heads = queries.reshape(row_count, KV_HEADS, group_size, HEAD_DIM)
    key_heads = self_keys.reshape(row_count, KV_HEADS, HEAD_DIM)
    value_heads = self_values.reshape(row_count, KV_HEADS, HEAD_DIM)
    results = []
    for kv_head in range(KV_HEADS):
        key_block = jnp.concatenate([doc_keys[:, kv_head], key_heads[:, kv_head]], 0).astype(jnp.float32)
        value_block = jnp.concatenate([doc_values[:, kv_head], value_heads[:, kv_head]], 0).astype(jnp.float32)
        scores = jnp.einsum("rgd,kd->rgk", query_heads[:, kv_head].astype(jnp.float32), key_block) * (HEAD_DIM ** -0.5)
        scores = jnp.where(visible[:, None, :], scores, -1e30)
        row_max = jnp.max(scores, -1)
        expos = jnp.exp(scores - row_max[..., None])
        totals = jnp.sum(expos, -1)
        weights = lax.optimization_barrier(expos.astype(jnp.bfloat16)).astype(jnp.float32)
        weighted = jnp.einsum("rgk,kd->rgd", weights, value_block)
        results.append((weighted / totals[..., None]).astype(jnp.bfloat16))
    attended = jnp.stack(results, 1).reshape(row_count, HEADS * HEAD_DIM)
    return jnp.dot(attended, w_out, preferred_element_type=jnp.float32).astype(jnp.bfloat16)
```

```python
import functools
import math

import jax
import jax.numpy as jnp
from jax import lax
from jax.experimental import pallas as pl
from jax.experimental.pallas import tpu as pltpu
from jax.sharding import PartitionSpec as P

CTX = 16
TP = 4
HEAD = 128
bf16 = jnp.bfloat16
f32 = jnp.float32


def dot(a, b):
    return jnp.dot(a, b, preferred_element_type=f32)


def dot_nt(a, b):
    return lax.dot_general(a, b, (((1,), (1,)), ((), ())), preferred_element_type=f32)


def project_kernel(t_ref, h0, h1, h2, h3, wq, wk, wv, out, acc):
    step = pl.program_id(0)
    for s, h in enumerate((h0, h1, h2, h3)):

        @pl.when(step == s)
        def _(h=h, s=s):
            rows = h[...]
            part = jnp.concatenate([dot(rows, wq[...]), dot(rows, wk[...]), dot(rows, wv[...])], 1)
            if s == 0:
                acc[...] = part
            elif s < TP - 1:
                acc[...] += part
            else:
                out[...] = (acc[...] + part).astype(bf16)


def project(t, pieces, w_query, w_key, w_value):
    rows, feats = pieces[0].shape
    width = w_query.shape[1] + w_key.shape[1] + w_value.shape[1]
    by_shift = lambda s, t: (lax.rem(t[0] + TP - s, TP), 0)
    fixed = lambda s, t: (0, 0)
    return pl.pallas_call(
        project_kernel,
        grid_spec=pltpu.PrefetchScalarGridSpec(
            num_scalar_prefetch=1,
            grid=(TP,),
            in_specs=[pl.BlockSpec((rows, feats), fixed)] * 4
            + [pl.BlockSpec((feats, w.shape[1]), by_shift) for w in (w_query, w_key, w_value)],
            out_specs=pl.BlockSpec((rows, width), fixed),
            scratch_shapes=[pltpu.VMEM((rows, width), f32)],
        ),
        out_shape=jax.ShapeDtypeStruct((rows, width), bf16),
        compiler_params=pltpu.CompilerParams(vmem_limit_bytes=24 * 2**20),
    )(t, *pieces, w_query, w_key, w_value)


def split3(x):
    hi = x.astype(bf16).astype(f32)
    mid = (x - hi).astype(bf16).astype(f32)
    return hi, mid, x - hi - mid


def attend_kernel(i_ref, q, kt, v, ks, vs, out, *, rows, chunk):
    step = pl.program_id(0)
    base = i_ref[0] * ks.shape[0]
    scale = (HEAD ** -0.5) * math.log2(math.e)
    groups = 4
    lane = lax.broadcasted_iota(jnp.int32, (rows, HEAD), 1)
    side = jnp.zeros((rows, HEAD), f32)
    keys = kt.shape[2]
    share = ks.shape[0]
    key_at = lax.broadcasted_iota(jnp.int32, (groups * rows, share), 1) + base
    row_at = lax.rem(lax.broadcasted_iota(jnp.int32, (groups * rows, share), 0), rows) + step * rows
    causal = key_at <= row_at
    ones = (lax.broadcasted_iota(jnp.int32, (share, HEAD), 1) == 0).astype(bf16)
    for kv in range(2):
        qh = jnp.concatenate(
            [q[:, (kv * groups + g) * HEAD : (kv * groups + g + 1) * HEAD] for g in range(groups)], 0
        )
        self_scores = dot_nt(qh, ks[:, kv * HEAD : (kv + 1) * HEAD])
        self_scores = jnp.where(causal, self_scores, -1e30)
        scores = [dot(qh, kt[kv, :, c : c + chunk]) for c in range(0, keys, chunk)]
        top = jnp.max(self_scores, -1, keepdims=True)
        for s in scores:
            top = jnp.maximum(top, jnp.max(s, -1, keepdims=True))
        weigh = lambda s: jnp.exp2((s - top) * scale).astype(bf16)
        acc = dot(weigh(self_scores), jnp.concatenate([vs[:, kv * HEAD : (kv + 1) * HEAD], ones], 1))
        for n, s in enumerate(scores):
            acc += dot(weigh(s), v[kv, n * chunk : (n + 1) * chunk, :])
        for g in range(groups):
            h = kv * groups + g
            part = acc[g * rows : (g + 1) * rows]
            out[:, h * HEAD : (h + 1) * HEAD] = part[:, :HEAD].astype(bf16)
            fields = split3(top[g * rows : (g + 1) * rows]) + split3(part[:, HEAD : HEAD + 1])
            for f, field in enumerate(fields):
                side = jnp.where(lane == f * 8 + h, field, side)
    out[:, 8 * HEAD : 9 * HEAD] = side.astype(bf16)


def attend(i, q, kt, v, ks, vs, rows=128, chunk=512):
    count, width = q.shape
    whole = lambda a: pl.BlockSpec(a.shape, lambda s, i: (0,) * a.ndim)
    return pl.pallas_call(
        functools.partial(attend_kernel, rows=rows, chunk=chunk),
        grid_spec=pltpu.PrefetchScalarGridSpec(
            num_scalar_prefetch=1,
            grid=(count // rows,),
            in_specs=[pl.BlockSpec((rows, width), lambda s, i: (s, 0))] + [whole(a) for a in (kt, v, ks, vs)],
            out_specs=pl.BlockSpec((rows, width + HEAD), lambda s, i: (s, 0)),
        ),
        out_shape=jax.ShapeDtypeStruct((count, width + HEAD), bf16),
        compiler_params=pltpu.CompilerParams(vmem_limit_bytes=40 * 2**20),
    )(i, q, kt, v, ks, vs)


def finish_kernel(t_ref, parts, w, out, att):
    scale = (HEAD ** -0.5) * math.log2(math.e)

    @pl.when(pl.program_id(0) == 0)
    def _():
        side = [parts[p, :, 8 * HEAD : 9 * HEAD].astype(f32) for p in range(CTX)]
        tops = [s[:, 0:8] + s[:, 8:16] + s[:, 16:24] for s in side]
        sums = [s[:, 24:32] + s[:, 32:40] + s[:, 40:48] for s in side]
        top = functools.reduce(jnp.maximum, tops)
        scales = [jnp.exp2((m - top) * scale) for m in tops]
        total = sum(a * b for a, b in zip(scales, sums))
        for h in range(8):
            acc = sum(
                parts[p, :, h * HEAD : (h + 1) * HEAD].astype(f32) * scales[p][:, h : h + 1] for p in range(CTX)
            )
            att[:, h * HEAD : (h + 1) * HEAD] = (acc / total[:, h : h + 1]).astype(bf16)

    out[0] = dot(att[...], w[...]).astype(bf16)


def finish(t, parts, w_out):
    _, share, width = parts.shape
    feats, cols = w_out.shape
    block = cols // TP
    return pl.pallas_call(
        finish_kernel,
        grid_spec=pltpu.PrefetchScalarGridSpec(
            num_scalar_prefetch=1,
            grid=(TP,),
            in_specs=[
                pl.BlockSpec(parts.shape, lambda s, t: (0, 0, 0)),
                pl.BlockSpec((feats, block), lambda s, t: (0, lax.rem(t[0] + s, TP))),
            ],
            out_specs=pl.BlockSpec((1, share, block), lambda s, t: (s, 0, 0)),
            scratch_shapes=[pltpu.VMEM((share, feats), bf16)],
        ),
        out_shape=jax.ShapeDtypeStruct((TP, share, block), bf16),
        compiler_params=pltpu.CompilerParams(vmem_limit_bytes=24 * 2**20),
    )(t, parts, w_out)


def shift(x, s):
    return lax.ppermute(x, "tp", [(i, (i + s) % TP) for i in range(TP)])


def local(response, owner, doc_lengths, doc_keys, doc_values, w_query, w_key, w_value, w_out):
    i = lax.axis_index("ctx").astype(jnp.int32).reshape(1)
    t = lax.axis_index("tp").astype(jnp.int32).reshape(1)
    count, feats = response.shape[1:]
    share = count // CTX
    cache = doc_keys.shape[0]
    visible = (jnp.arange(cache) < doc_lengths[0])[:, None, None]
    keys_t = jnp.where(visible, doc_keys, doc_keys[:1]).transpose(1, 2, 0)
    side = jnp.broadcast_to((jnp.arange(HEAD) == 0)[None, None, :], doc_values.shape).astype(bf16)
    values = jnp.where(visible, jnp.concatenate([doc_values, side], 2), 0).transpose(1, 0, 2)

    chunks = lax.all_to_all(response[0].reshape(CTX, share, feats), "ctx", 0, 0)
    mine = lax.dynamic_index_in_dim(chunks, owner[0], 0, keepdims=False)
    pieces = [mine] + [shift(mine, s) for s in range(1, TP)]
    qkv = project(t, pieces, w_query, w_key, w_value)
    width = w_query.shape[1]
    kv_width = w_key.shape[1]
    queries = lax.all_to_all(jnp.broadcast_to(qkv[None, :, :width], (CTX, share, width)), "ctx", 0, 0)
    sent = attend(
        i,
        queries.reshape(count, width),
        keys_t,
        values,
        qkv[:, width : width + kv_width],
        qkv[:, width + kv_width :],
    )
    parts = lax.all_to_all(sent.reshape(CTX, share, width + HEAD), "ctx", 0, 0)
    partial_out = finish(t, parts, w_out)
    out = partial_out[0].astype(f32)
    for s in range(1, TP):
        out += shift(partial_out[s], s).astype(f32)
    return out.astype(bf16)


def solution(mesh):
    placed = (
        P(("dp", "ctx"), None, "tp"),
        P("dp"),
        P(("dp", "ctx")),
        P(("dp", "ctx"), "tp", None),
        P(("dp", "ctx"), "tp", None),
        P(None, "tp"),
        P(None, "tp"),
        P(None, "tp"),
        P("tp", None),
    )
    return jax.shard_map(
        local, mesh=mesh, in_specs=placed, out_specs=P(("dp", "ctx"), "tp"), check_vma=False
    )
```

```python
import functools
import math

import jax
import jax.numpy as jnp
from jax import lax
from jax.experimental import pallas as pl
from jax.experimental.pallas import tpu as pltpu
from jax.sharding import PartitionSpec as P

CTX = 16
TP = 4
HEAD = 128
bf16 = jnp.bfloat16
f32 = jnp.float32


def dot(a, b):
    return jnp.dot(a, b, preferred_element_type=f32)


def dot_nt(a, b):
    return lax.dot_general(a, b, (((1,), (1,)), ((), ())), preferred_element_type=f32)


def begin_kernel(h, wk, wv, keys, values):
    feats = h.shape[1]
    start = pl.multiple_of(lax.axis_index("tp") * feats, feats)
    for w, out in ((wk, keys), (wv, values)):
        out[...] = dot(h[...], w[pl.ds(start, feats), :])


def begin(mine, w_key, w_value):
    vmem = pl.BlockSpec(memory_space=pltpu.VMEM)
    return pl.pallas_call(
        begin_kernel,
        in_specs=[vmem] * 3,
        out_specs=[vmem] * 2,
        out_shape=[jax.ShapeDtypeStruct((mine.shape[0], w.shape[1]), f32) for w in (w_key, w_value)],
        compiler_params=pltpu.CompilerParams(vmem_limit_bytes=6 * 2**20),
        cost_estimate=pl.CostEstimate(flops=0, bytes_accessed=48 * 2**20, transcendentals=0),
    )(mine, w_key, w_value)


def project_kernel(h0, h1, h2, h3, k0, v0, wq, wk, wv, queries, keys, values):
    feats = h0.shape[1]
    totals = [0.0, k0[...], v0[...]]
    for s, h in enumerate((h0, h1, h2, h3)):
        start = pl.multiple_of(lax.rem(lax.axis_index("tp") + TP - s, TP) * feats, feats)
        rows = h[...]
        for m, w in enumerate((wq, wk, wv)):
            if s > 0 or m == 0:
                totals[m] = totals[m] + dot(rows, w[pl.ds(start, feats), :])
    q = totals[0].astype(bf16)
    for c in range(CTX):
        queries[c] = q
    keys[...] = totals[1].astype(bf16)
    values[...] = totals[2].astype(bf16)


def project(pieces, begun, w_query, w_key, w_value):
    rows, feats = pieces[0].shape
    vmem = pl.BlockSpec(memory_space=pltpu.VMEM)
    shapes = [(CTX, rows, w_query.shape[1]), (rows, w_key.shape[1]), (rows, w_value.shape[1])]
    return pl.pallas_call(
        project_kernel,
        in_specs=[vmem] * 9,
        out_specs=[vmem] * 3,
        out_shape=[jax.ShapeDtypeStruct(s, bf16) for s in shapes],
        compiler_params=pltpu.CompilerParams(vmem_limit_bytes=6 * 2**20),
    )(*pieces, *begun, w_query, w_key, w_value)


def split3(x):
    hi = x.astype(bf16).astype(f32)
    mid = (x - hi).astype(bf16).astype(f32)
    return hi, mid, x - hi - mid


def attend_kernel(len_ref, q, k, v, ks, vs, out, *, rows, chunk):
    scale = (HEAD ** -0.5) * math.log2(math.e)
    groups = 4
    keys = k.shape[1]
    share = ks.shape[0]
    starts = range(0, keys, chunk)
    units = [(r, kv) for r in range(0, q.shape[0], rows) for kv in range(2)]
    lane = lax.broadcasted_iota(jnp.int32, (rows, HEAD), 1)
    key_at = lax.broadcasted_iota(jnp.int32, (groups * rows, share), 1) + lax.axis_index("ctx") * share
    row_at = lax.rem(lax.broadcasted_iota(jnp.int32, (groups * rows, share), 0), rows)
    ones = (lax.broadcasted_iota(jnp.int32, (share, HEAD), 1) == 0).astype(bf16)
    chunk_at = lax.broadcasted_iota(jnp.int32, (chunk, HEAD), 0)
    chunk_lane = lax.broadcasted_iota(jnp.int32, (chunk, HEAD), 1)
    counted = [
        jnp.where((chunk_at < len_ref[0] - c) & (chunk_lane == 0), 1.0, 0.0).astype(bf16) for c in starts
    ]

    def heads_of(r, kv):
        cols = [(kv * groups + g) * HEAD for g in range(groups)]
        return jnp.concatenate([q[r : r + rows, c : c + HEAD] for c in cols], 0)

    def of_kv(ref, kv):
        return ref[:, kv * HEAD : (kv + 1) * HEAD]

    heads = heads_of(*units[0])
    scores = [dot_nt(heads, k[0, c : c + chunk, :]) for c in starts]
    for n, (r, kv) in enumerate(units):
        self_scores = jnp.where(key_at <= row_at + r, dot_nt(heads, of_kv(ks, kv)), -1e30)
        tops = [s[:, c : c + HEAD] for s in scores for c in range(0, chunk, HEAD)]
        top = jnp.max(functools.reduce(jnp.maximum, tops), -1, keepdims=True)
        top = jnp.maximum(top, jnp.max(self_scores, -1, keepdims=True))
        weigh = lambda s: jnp.exp2((s - top) * scale).astype(bf16)
        acc = dot(weigh(self_scores), jnp.concatenate([of_kv(vs, kv), ones], 1))
        after = units[n + 1] if n + 1 < len(units) else None
        if after:
            heads = heads_of(*after)
        upcoming = []
        for c, s, count in zip(starts, scores, counted):
            if after:
                upcoming.append(dot_nt(heads, k[after[1], c : c + chunk, :]))
            acc += dot(weigh(s), jnp.concatenate([v[kv, c : c + chunk, :], count], 1))
        scores = upcoming
        if kv == 0:
            tops_at = sums_at = jnp.zeros((rows, HEAD), f32)
        for g in range(groups):
            h = kv * groups + g
            part = acc[g * rows : (g + 1) * rows]
            out[r : r + rows, h * HEAD : (h + 1) * HEAD] = part[:, :HEAD].astype(bf16)
            tops_at = jnp.where(lane == h, top[g * rows : (g + 1) * rows], tops_at)
            sums_at = jnp.where(lane == h, part[:, HEAD : HEAD + 1], sums_at)
        if kv == 1:
            fields = split3(tops_at) + split3(sums_at)
            side = fields[0] + sum(pltpu.roll(x, 8 * f, 1) for f, x in enumerate(fields) if f)
            out[r : r + rows, 8 * HEAD : 9 * HEAD] = side.astype(bf16)


def attend(length, q, k, v, ks, vs, rows=128, chunk=512):
    count, width = q.shape
    vmem = pl.BlockSpec(memory_space=pltpu.VMEM)
    smem = pl.BlockSpec(memory_space=pltpu.SMEM)
    return pl.pallas_call(
        functools.partial(attend_kernel, rows=rows, chunk=chunk),
        in_specs=[smem] + [vmem] * 5,
        out_specs=vmem,
        out_shape=jax.ShapeDtypeStruct((count, width + HEAD), bf16),
        compiler_params=pltpu.CompilerParams(vmem_limit_bytes=24 * 2**20),
        cost_estimate=pl.CostEstimate(flops=0, bytes_accessed=32 * 2**20, transcendentals=0),
    )(length, q, k, v, ks, vs)


def finish_kernel(parts, w, out):
    scale = (HEAD ** -0.5) * math.log2(math.e)
    block = out.shape[2]
    starts = [pl.multiple_of(lax.rem(lax.axis_index("tp") + s, TP) * block, block) for s in range(TP)]
    side = [parts[p, :, 8 * HEAD : 9 * HEAD].astype(f32) for p in range(CTX)]
    tops = [s[:, 0:8] + s[:, 8:16] + s[:, 16:24] for s in side]
    sums = [s[:, 24:32] + s[:, 32:40] + s[:, 40:48] for s in side]
    top = functools.reduce(jnp.maximum, tops)
    scales = [jnp.exp2((m - top) * scale) for m in tops]
    total = sum(a * b for a, b in zip(scales, sums))
    heads = []
    for h in range(8):
        acc = sum(parts[p, :, h * HEAD : (h + 1) * HEAD].astype(f32) * scales[p][:, h : h + 1] for p in range(CTX))
        heads.append((acc / total[:, h : h + 1]).astype(bf16))
    attended = jnp.concatenate(heads, 1)
    for s in range(TP):
        out[s] = dot(attended, w[:, pl.ds(starts[s], block)]).astype(bf16)


def finish(parts, w_out):
    _, share, width = parts.shape
    feats, cols = w_out.shape
    block = cols // TP
    vmem = pl.BlockSpec(memory_space=pltpu.VMEM)
    return pl.pallas_call(
        finish_kernel,
        in_specs=[vmem, vmem],
        out_specs=vmem,
        out_shape=jax.ShapeDtypeStruct((TP, share, block), bf16),
        compiler_params=pltpu.CompilerParams(vmem_limit_bytes=6 * 2**20),
        cost_estimate=pl.CostEstimate(
            flops=2 * share * feats * cols, bytes_accessed=2 * w_out.size, transcendentals=0
        ),
    )(parts, w_out)


def shift(x, s):
    return lax.ppermute(x, "tp", [(i, (i + s) % TP) for i in range(TP)])


def local(response, owner, doc_lengths, doc_keys, doc_values, w_query, w_key, w_value, w_out):
    count, feats = response.shape[1:]
    share = count // CTX
    cache = doc_keys.shape[0]
    chunks = lax.all_to_all(response[0].reshape(CTX, share, feats), "ctx", 0, 0)
    chunks, owner, doc_lengths, doc_keys, doc_values = lax.optimization_barrier(
        (chunks, owner, doc_lengths, doc_keys, doc_values)
    )
    mine = lax.dynamic_index_in_dim(chunks, owner[0], 0, keepdims=False)
    pieces = [mine] + [shift(mine, s) for s in range(1, TP)]
    visible = (jnp.arange(cache) < doc_lengths[0])[:, None, None]
    keys = jnp.where(visible, doc_keys, doc_keys[:1]).transpose(1, 0, 2)
    values = jnp.where(visible, doc_values, 0).transpose(1, 0, 2)
    begun = begin(mine, w_key, w_value)
    queries, self_keys, self_values = project(pieces, begun, w_query, w_key, w_value)
    queries, keys, values, self_keys, self_values, doc_lengths = lax.optimization_barrier(
        (queries, keys, values, self_keys, self_values, doc_lengths)
    )
    queries = lax.all_to_all(queries, "ctx", 0, 0).reshape(count, -1)
    sent = attend(doc_lengths, queries, keys, values, self_keys, self_values)
    parts = lax.all_to_all(sent.reshape(CTX, share, -1), "ctx", 0, 0)
    partial_out = finish(parts, w_out)
    out = partial_out[0].astype(f32)
    for s in range(1, TP):
        out += shift(partial_out[s], s).astype(f32)
    return out.astype(bf16)


def solution(mesh):
    placed = (
        P(("dp", "ctx"), None, "tp"),
        P("dp"),
        P(("dp", "ctx")),
        P(("dp", "ctx"), "tp", None),
        P(("dp", "ctx"), "tp", None),
        P(None, "tp"),
        P(None, "tp"),
        P(None, "tp"),
        P("tp", None),
    )
    return jax.shard_map(
        local, mesh=mesh, in_specs=placed, out_specs=P(("dp", "ctx"), "tp"), check_vma=False
    )
```

```python
import functools
import math

import jax
import jax.numpy as jnp
from jax import lax
from jax.experimental import pallas as pl
from jax.experimental.pallas import tpu as pltpu
from jax.sharding import PartitionSpec as P

CTX = 16
TP = 4
HEAD = 128
bf16 = jnp.bfloat16
f32 = jnp.float32


def dot(a, b):
    return jnp.dot(a, b, preferred_element_type=f32)


def dot_nt(a, b):
    return lax.dot_general(a, b, (((1,), (1,)), ((), ())), preferred_element_type=f32)


def begin_kernel(h, wk, wv, ready, keys, values):
    feats = h.shape[1]
    start = pl.multiple_of(lax.axis_index("tp") * feats, feats)
    for w, out in ((wk, keys), (wv, values)):
        out[...] = dot(h[...], w[pl.ds(start, feats), :])


def begin(mine, w_key, w_value, ready):
    vmem = pl.BlockSpec(memory_space=pltpu.VMEM)
    return pl.pallas_call(
        begin_kernel,
        in_specs=[vmem] * 3 + [pl.BlockSpec(memory_space=pl.ANY)],
        out_specs=[vmem] * 2,
        out_shape=[jax.ShapeDtypeStruct((mine.shape[0], w.shape[1]), f32) for w in (w_key, w_value)],
        compiler_params=pltpu.CompilerParams(vmem_limit_bytes=6 * 2**20),
        cost_estimate=pl.CostEstimate(flops=0, bytes_accessed=48 * 2**20, transcendentals=0),
    )(mine, w_key, w_value, ready)


def project_kernel(h0, h1, h2, h3, k0, v0, wq, wk, wv, queries, keys, values):
    feats = h0.shape[1]
    totals = [0.0, k0[...], v0[...]]
    for s, h in enumerate((h0, h1, h2, h3)):
        start = pl.multiple_of(lax.rem(lax.axis_index("tp") + TP - s, TP) * feats, feats)
        rows = h[...]
        for m, w in enumerate((wq, wk, wv)):
            if s > 0 or m == 0:
                totals[m] = totals[m] + dot(rows, w[pl.ds(start, feats), :])
    q = totals[0].astype(bf16)
    for c in range(CTX):
        queries[c] = q
    keys[...] = totals[1].astype(bf16)
    values[...] = totals[2].astype(bf16)


def project(pieces, begun, w_query, w_key, w_value):
    rows, feats = pieces[0].shape
    vmem = pl.BlockSpec(memory_space=pltpu.VMEM)
    shapes = [(CTX, rows, w_query.shape[1]), (rows, w_key.shape[1]), (rows, w_value.shape[1])]
    return pl.pallas_call(
        project_kernel,
        in_specs=[vmem] * 9,
        out_specs=[vmem] * 3,
        out_shape=[jax.ShapeDtypeStruct(s, bf16) for s in shapes],
        compiler_params=pltpu.CompilerParams(vmem_limit_bytes=6 * 2**20),
    )(*pieces, *begun, w_query, w_key, w_value)


def split3(x):
    hi = x.astype(bf16).astype(f32)
    mid = (x - hi).astype(bf16).astype(f32)
    return hi, mid, x - hi - mid


def attend_kernel(len_ref, q, k, v, ks, vs, out, *, rows, chunk):
    scale = (HEAD ** -0.5) * math.log2(math.e)
    groups = 4
    keys = k.shape[1]
    share = ks.shape[0]
    starts = range(0, keys, chunk)
    units = [(r, kv) for r in range(0, q.shape[0], rows) for kv in range(2)]
    lane = lax.broadcasted_iota(jnp.int32, (rows, HEAD), 1)
    key_at = lax.broadcasted_iota(jnp.int32, (groups * rows, share), 1) + lax.axis_index("ctx") * share
    row_at = lax.rem(lax.broadcasted_iota(jnp.int32, (groups * rows, share), 0), rows)
    ones = (lax.broadcasted_iota(jnp.int32, (share, HEAD), 1) == 0).astype(bf16)
    chunk_at = lax.broadcasted_iota(jnp.int32, (chunk, HEAD), 0)
    chunk_lane = lax.broadcasted_iota(jnp.int32, (chunk, HEAD), 1)
    counted = [
        jnp.where((chunk_at < len_ref[0] - c) & (chunk_lane == 0), 1.0, 0.0).astype(bf16) for c in starts
    ]

    def heads_of(r, kv):
        cols = [(kv * groups + g) * HEAD for g in range(groups)]
        return jnp.concatenate([q[r : r + rows, c : c + HEAD] for c in cols], 0)

    def of_kv(ref, kv):
        return ref[:, kv * HEAD : (kv + 1) * HEAD]

    heads = heads_of(*units[0])
    scores = [dot_nt(heads, k[0, c : c + chunk, :]) for c in starts]
    for n, (r, kv) in enumerate(units):
        self_scores = jnp.where(key_at <= row_at + r, dot_nt(heads, of_kv(ks, kv)), -1e30)
        tops = [s[:, c : c + HEAD] for s in scores for c in range(0, chunk, HEAD)]
        top = jnp.max(functools.reduce(jnp.maximum, tops), -1, keepdims=True)
        top = jnp.maximum(top, jnp.max(self_scores, -1, keepdims=True))
        weigh = lambda s: jnp.exp2((s - top) * scale).astype(bf16)
        acc = dot(weigh(self_scores), jnp.concatenate([of_kv(vs, kv), ones], 1))
        after = units[n + 1] if n + 1 < len(units) else None
        if after:
            heads = heads_of(*after)
        upcoming = []
        for c, s, count in zip(starts, scores, counted):
            if after:
                upcoming.append(dot_nt(heads, k[after[1], c : c + chunk, :]))
            acc += dot(weigh(s), jnp.concatenate([v[kv, c : c + chunk, :], count], 1))
        scores = upcoming
        if kv == 0:
            tops_at = sums_at = jnp.zeros((rows, HEAD), f32)
        for g in range(groups):
            h = kv * groups + g
            part = acc[g * rows : (g + 1) * rows]
            out[r : r + rows, h * HEAD : (h + 1) * HEAD] = part[:, :HEAD].astype(bf16)
            tops_at = jnp.where(lane == h, top[g * rows : (g + 1) * rows], tops_at)
            sums_at = jnp.where(lane == h, part[:, HEAD : HEAD + 1], sums_at)
        if kv == 1:
            fields = split3(tops_at) + split3(sums_at)
            side = fields[0] + sum(pltpu.roll(x, 8 * f, 1) for f, x in enumerate(fields) if f)
            out[r : r + rows, 8 * HEAD : 9 * HEAD] = side.astype(bf16)


def attend(length, q, k, v, ks, vs, rows=128, chunk=512):
    count, width = q.shape
    vmem = pl.BlockSpec(memory_space=pltpu.VMEM)
    smem = pl.BlockSpec(memory_space=pltpu.SMEM)
    return pl.pallas_call(
        functools.partial(attend_kernel, rows=rows, chunk=chunk),
        in_specs=[smem] + [vmem] * 5,
        out_specs=vmem,
        out_shape=jax.ShapeDtypeStruct((count, width + HEAD), bf16),
        compiler_params=pltpu.CompilerParams(vmem_limit_bytes=24 * 2**20),
        cost_estimate=pl.CostEstimate(flops=0, bytes_accessed=32 * 2**20, transcendentals=0),
    )(length, q, k, v, ks, vs)


def finish_kernel(parts, w, *outs, shifts):
    scale = (HEAD ** -0.5) * math.log2(math.e)
    side = [parts[p, :, 8 * HEAD : 9 * HEAD].astype(f32) for p in range(CTX)]
    tops = [s[:, 0:8] + s[:, 8:16] + s[:, 16:24] for s in side]
    sums = [s[:, 24:32] + s[:, 32:40] + s[:, 40:48] for s in side]
    top = functools.reduce(jnp.maximum, tops)
    scales = [jnp.exp2((m - top) * scale) for m in tops]
    total = sum(a * b for a, b in zip(scales, sums))
    heads = []
    for h in range(8):
        acc = sum(parts[p, :, h * HEAD : (h + 1) * HEAD].astype(f32) * scales[p][:, h : h + 1] for p in range(CTX))
        heads.append((acc / total[:, h : h + 1]).astype(bf16))
    attended = jnp.concatenate(heads, 1)
    block = outs[0].shape[1]
    for s, out in zip(shifts, outs):
        start = pl.multiple_of(lax.rem(lax.axis_index("tp") + s, TP) * block, block)
        out[...] = dot(attended, w[:, pl.ds(start, block)]).astype(bf16)


def finish(parts, w_out, shifts):
    share = parts.shape[1]
    block = w_out.shape[1] // TP
    vmem = pl.BlockSpec(memory_space=pltpu.VMEM)
    return pl.pallas_call(
        functools.partial(finish_kernel, shifts=shifts),
        in_specs=[vmem] * 2,
        out_specs=[vmem] * len(shifts),
        out_shape=[jax.ShapeDtypeStruct((share, block), bf16) for _ in shifts],
        compiler_params=pltpu.CompilerParams(vmem_limit_bytes=6 * 2**20),
        cost_estimate=pl.CostEstimate(
            flops=2 * share * w_out.size, bytes_accessed=2 * w_out.size, transcendentals=0
        ),
    )(parts, w_out)


def shift(x, s):
    return lax.ppermute(x, "tp", [(i, (i + s) % TP) for i in range(TP)])


def local(response, owner, doc_lengths, doc_keys, doc_values, w_query, w_key, w_value, w_out):
    count, feats = response.shape[1:]
    share = count // CTX
    cache = doc_keys.shape[0]
    chunks = lax.all_to_all(response[0].reshape(CTX, share, feats), "ctx", 0, 0)
    chunks, owner, doc_lengths, doc_keys, doc_values = lax.optimization_barrier(
        (chunks, owner, doc_lengths, doc_keys, doc_values)
    )
    mine = lax.dynamic_index_in_dim(chunks, owner[0], 0, keepdims=False)
    pieces = [mine] + [shift(mine, s) for s in range(1, TP)]
    visible = (jnp.arange(cache) < doc_lengths[0])[:, None, None]
    keys = jnp.where(visible, doc_keys, doc_keys[:1]).transpose(1, 0, 2)
    values = jnp.where(visible, doc_values, 0).transpose(1, 0, 2)
    begun = begin(mine, w_key, w_value, keys)
    queries, self_keys, self_values = project(pieces, begun, w_query, w_key, w_value)
    queries, keys, values, self_keys, self_values, doc_lengths = lax.optimization_barrier(
        (queries, keys, values, self_keys, self_values, doc_lengths)
    )
    queries = lax.all_to_all(queries, "ctx", 0, 0).reshape(count, -1)
    sent = attend(doc_lengths, queries, keys, values, self_keys, self_values)
    parts = lax.all_to_all(sent.reshape(CTX, share, -1), "ctx", 0, 0)
    *away, own = finish(parts, w_out, (2, 1, 3, 0))
    away = [shift(x, s) for x, s in zip(away, (2, 1, 3))]
    return sum(x.astype(f32) for x in (own, *away)).astype(bf16)


def solution(mesh):
    placed = (
        P(("dp", "ctx"), None, "tp"),
        P("dp"),
        P(("dp", "ctx")),
        P(("dp", "ctx"), "tp", None),
        P(("dp", "ctx"), "tp", None),
        P(None, "tp"),
        P(None, "tp"),
        P(None, "tp"),
        P("tp", None),
    )
    return jax.shard_map(
        local, mesh=mesh, in_specs=placed, out_specs=P(("dp", "ctx"), "tp"), check_vma=False
    )
```

```python
import functools
import math

import jax
import jax.numpy as jnp
from jax import lax
from jax.experimental import pallas as pl
from jax.experimental.pallas import tpu as pltpu
from jax.sharding import PartitionSpec as P

CTX = 16
TP = 4
HEAD = 128
bf16 = jnp.bfloat16
f32 = jnp.float32


def dot(a, b):
    return jnp.dot(a, b, preferred_element_type=f32)


def dot_nt(a, b):
    return lax.dot_general(a, b, (((1,), (1,)), ((), ())), preferred_element_type=f32)


def begin_kernel(h, wk, wv, ready, keys, values):
    feats = h.shape[1]
    start = pl.multiple_of(lax.axis_index("tp") * feats, feats)
    for w, out in ((wk, keys), (wv, values)):
        out[...] = dot(h[...], w[pl.ds(start, feats), :])


def begin(mine, w_key, w_value, ready):
    vmem = pl.BlockSpec(memory_space=pltpu.VMEM)
    return pl.pallas_call(
        begin_kernel,
        in_specs=[vmem] * 3 + [pl.BlockSpec(memory_space=pl.ANY)],
        out_specs=[vmem] * 2,
        out_shape=[jax.ShapeDtypeStruct((mine.shape[0], w.shape[1]), f32) for w in (w_key, w_value)],
        compiler_params=pltpu.CompilerParams(vmem_limit_bytes=6 * 2**20),
        cost_estimate=pl.CostEstimate(flops=0, bytes_accessed=48 * 2**20, transcendentals=0),
    )(mine, w_key, w_value, ready)


def project_kernel(h0, h1, h2, h3, k0, v0, wq, wk, wv, queries, keys, values):
    feats = h0.shape[1]
    totals = [0.0, k0[...], v0[...]]
    for s, h in enumerate((h0, h1, h2, h3)):
        start = pl.multiple_of(lax.rem(lax.axis_index("tp") + TP - s, TP) * feats, feats)
        rows = h[...]
        for m, w in enumerate((wq, wk, wv)):
            if s > 0 or m == 0:
                totals[m] = totals[m] + dot(rows, w[pl.ds(start, feats), :])
    q = totals[0].astype(bf16)
    for c in range(CTX):
        queries[c] = q
    keys[...] = totals[1].astype(bf16)
    values[...] = totals[2].astype(bf16)


def project(pieces, begun, w_query, w_key, w_value):
    rows, feats = pieces[0].shape
    vmem = pl.BlockSpec(memory_space=pltpu.VMEM)
    shapes = [(CTX, rows, w_query.shape[1]), (rows, w_key.shape[1]), (rows, w_value.shape[1])]
    return pl.pallas_call(
        project_kernel,
        in_specs=[vmem] * 9,
        out_specs=[vmem] * 3,
        out_shape=[jax.ShapeDtypeStruct(s, bf16) for s in shapes],
        compiler_params=pltpu.CompilerParams(vmem_limit_bytes=6 * 2**20),
    )(*pieces, *begun, w_query, w_key, w_value)


def split3(x):
    hi = x.astype(bf16).astype(f32)
    mid = (x - hi).astype(bf16).astype(f32)
    return hi, mid, x - hi - mid


def attend_kernel(len_ref, q, k, v, ks, vs, out, *, rows, chunk):
    scale = (HEAD ** -0.5) * math.log2(math.e)
    groups = 4
    keys = k.shape[1]
    share = ks.shape[0]
    starts = range(0, keys, chunk)
    units = [(r, kv) for r in range(0, q.shape[0], rows) for kv in range(2)]
    lane = lax.broadcasted_iota(jnp.int32, (rows, HEAD), 1)
    key_at = lax.broadcasted_iota(jnp.int32, (groups * rows, share), 1) + lax.axis_index("ctx") * share
    row_at = lax.rem(lax.broadcasted_iota(jnp.int32, (groups * rows, share), 0), rows)
    ones = (lax.broadcasted_iota(jnp.int32, (share, HEAD), 1) == 0).astype(bf16)
    chunk_at = lax.broadcasted_iota(jnp.int32, (chunk, HEAD), 0)
    chunk_lane = lax.broadcasted_iota(jnp.int32, (chunk, HEAD), 1)
    counted = [
        jnp.where((chunk_at < len_ref[0] - c) & (chunk_lane == 0), 1.0, 0.0).astype(bf16) for c in starts
    ]
    hidden = [jnp.where(chunk_at < len_ref[0] - c, 0.0, 1.0).astype(bf16) for c in starts]
    fill = [[gone * k[kv, 0:1, :] for gone in hidden] for kv in range(2)]

    def keys_of(kv, n):
        block = k[kv, n * chunk : (n + 1) * chunk, :]
        return block + fill[kv][n] if n else block

    def heads_of(r, kv):
        cols = [(kv * groups + g) * HEAD for g in range(groups)]
        return jnp.concatenate([q[r : r + rows, c : c + HEAD] for c in cols], 0)

    def of_kv(ref, kv):
        return ref[:, kv * HEAD : (kv + 1) * HEAD]

    heads = heads_of(*units[0])
    scores = [dot_nt(heads, keys_of(0, n)) for n in range(len(starts))]
    for n, (r, kv) in enumerate(units):
        self_scores = jnp.where(key_at <= row_at + r, dot_nt(heads, of_kv(ks, kv)), -1e30)
        tops = [s[:, c : c + HEAD] for s in scores for c in range(0, chunk, HEAD)]
        top = jnp.max(functools.reduce(jnp.maximum, tops), -1, keepdims=True)
        top = jnp.maximum(top, jnp.max(self_scores, -1, keepdims=True))
        weigh = lambda s: jnp.exp2((s - top) * scale).astype(bf16)
        acc = dot(weigh(self_scores), jnp.concatenate([of_kv(vs, kv), ones], 1))
        after = units[n + 1] if n + 1 < len(units) else None
        if after:
            heads = heads_of(*after)
        upcoming = []
        for m, (c, s, count) in enumerate(zip(starts, scores, counted)):
            if after:
                upcoming.append(dot_nt(heads, keys_of(after[1], m)))
            acc += dot(weigh(s), jnp.concatenate([v[kv, c : c + chunk, :], count], 1))
        scores = upcoming
        if kv == 0:
            tops_at = sums_at = jnp.zeros((rows, HEAD), f32)
        for g in range(groups):
            h = kv * groups + g
            part = acc[g * rows : (g + 1) * rows]
            out[r : r + rows, h * HEAD : (h + 1) * HEAD] = part[:, :HEAD].astype(bf16)
            tops_at = jnp.where(lane == h, top[g * rows : (g + 1) * rows], tops_at)
            sums_at = jnp.where(lane == h, part[:, HEAD : HEAD + 1], sums_at)
        if kv == 1:
            fields = split3(tops_at) + split3(sums_at)
            side = fields[0] + sum(pltpu.roll(x, 8 * f, 1) for f, x in enumerate(fields) if f)
            out[r : r + rows, 8 * HEAD : 9 * HEAD] = side.astype(bf16)


def attend(length, q, k, v, ks, vs, rows=128, chunk=512):
    count, width = q.shape
    vmem = pl.BlockSpec(memory_space=pltpu.VMEM)
    smem = pl.BlockSpec(memory_space=pltpu.SMEM)
    return pl.pallas_call(
        functools.partial(attend_kernel, rows=rows, chunk=chunk),
        in_specs=[smem] + [vmem] * 5,
        out_specs=vmem,
        out_shape=jax.ShapeDtypeStruct((count, width + HEAD), bf16),
        compiler_params=pltpu.CompilerParams(vmem_limit_bytes=24 * 2**20),
        cost_estimate=pl.CostEstimate(flops=0, bytes_accessed=32 * 2**20, transcendentals=0),
    )(length, q, k, v, ks, vs)


def finish_kernel(parts, w, *outs, shifts):
    scale = (HEAD ** -0.5) * math.log2(math.e)
    side = [parts[p, :, 8 * HEAD : 9 * HEAD].astype(f32) for p in range(CTX)]
    tops = [s[:, 0:8] + s[:, 8:16] + s[:, 16:24] for s in side]
    sums = [s[:, 24:32] + s[:, 32:40] + s[:, 40:48] for s in side]
    top = functools.reduce(jnp.maximum, tops)
    scales = [jnp.exp2((m - top) * scale) for m in tops]
    total = sum(a * b for a, b in zip(scales, sums))
    block = outs[0].shape[1]
    starts = [pl.multiple_of(lax.rem(lax.axis_index("tp") + s, TP) * block, block) for s in shifts]
    sums_out = [0.0] * len(shifts)
    for first in range(0, 8, 2):
        heads = []
        for h in (first, first + 1):
            acc = sum(
                parts[p, :, h * HEAD : (h + 1) * HEAD].astype(f32) * scales[p][:, h : h + 1] for p in range(CTX)
            )
            heads.append((acc / total[:, h : h + 1]).astype(bf16))
        attended = jnp.concatenate(heads, 1)
        rows = pl.ds(first * HEAD, 2 * HEAD)
        sums_out = [o + dot(attended, w[rows, pl.ds(c, block)]) for o, c in zip(sums_out, starts)]
    for out, value in zip(outs, sums_out):
        out[...] = value.astype(bf16)


def finish(parts, w_out, shifts):
    share = parts.shape[1]
    block = w_out.shape[1] // TP
    vmem = pl.BlockSpec(memory_space=pltpu.VMEM)
    return pl.pallas_call(
        functools.partial(finish_kernel, shifts=shifts),
        in_specs=[vmem] * 2,
        out_specs=[vmem] * len(shifts),
        out_shape=[jax.ShapeDtypeStruct((share, block), bf16) for _ in shifts],
        compiler_params=pltpu.CompilerParams(vmem_limit_bytes=6 * 2**20),
        cost_estimate=pl.CostEstimate(
            flops=2 * share * w_out.size, bytes_accessed=2 * w_out.size, transcendentals=0
        ),
    )(parts, w_out)


def shift(x, s):
    return lax.ppermute(x, "tp", [(i, (i + s) % TP) for i in range(TP)])


def local(response, owner, doc_lengths, doc_keys, doc_values, w_query, w_key, w_value, w_out):
    count, feats = response.shape[1:]
    share = count // CTX
    cache = doc_keys.shape[0]
    chunks = lax.all_to_all(response[0].reshape(CTX, share, feats), "ctx", 0, 0)
    chunks, owner, doc_lengths, doc_keys, doc_values = lax.optimization_barrier(
        (chunks, owner, doc_lengths, doc_keys, doc_values)
    )
    mine = lax.dynamic_index_in_dim(chunks, owner[0], 0, keepdims=False)
    pieces = [mine] + [shift(mine, s) for s in range(1, TP)]
    visible = (jnp.arange(cache) < doc_lengths[0])[:, None, None]
    keys = jnp.where(visible, doc_keys, 0).transpose(1, 0, 2)
    values = jnp.where(visible, doc_values, 0).transpose(1, 0, 2)
    begun = begin(mine, w_key, w_value, keys)
    queries, self_keys, self_values = project(pieces, begun, w_query, w_key, w_value)
    queries, keys, values, self_keys, self_values, doc_lengths = lax.optimization_barrier(
        (queries, keys, values, self_keys, self_values, doc_lengths)
    )
    queries = lax.all_to_all(queries, "ctx", 0, 0).reshape(count, -1)
    sent = attend(doc_lengths, queries, keys, values, self_keys, self_values)
    parts = lax.all_to_all(sent.reshape(CTX, share, -1), "ctx", 0, 0)
    *away, own = finish(parts, w_out, (2, 1, 3, 0))
    away = [shift(x, s) for x, s in zip(away, (2, 1, 3))]
    return sum(x.astype(f32) for x in (own, *away)).astype(bf16)


def solution(mesh):
    placed = (
        P(("dp", "ctx"), None, "tp"),
        P("dp"),
        P(("dp", "ctx")),
        P(("dp", "ctx"), "tp", None),
        P(("dp", "ctx"), "tp", None),
        P(None, "tp"),
        P(None, "tp"),
        P(None, "tp"),
        P("tp", None),
    )
    return jax.shard_map(
        local, mesh=mesh, in_specs=placed, out_specs=P(("dp", "ctx"), "tp"), check_vma=False
    )
```

```python
import functools
import math

import jax
import jax.numpy as jnp
from jax import lax
from jax.experimental import pallas as pl
from jax.experimental.pallas import tpu as pltpu
from jax.sharding import PartitionSpec as P

CTX = 16
TP = 4
HEAD = 128
bf16 = jnp.bfloat16
f32 = jnp.float32


def dot(a, b):
    return jnp.dot(a, b, preferred_element_type=f32)


def dot_nt(a, b):
    return lax.dot_general(a, b, (((1,), (1,)), ((), ())), preferred_element_type=f32)


def begin_kernel(h, wk, wv, ready, keys, values):
    feats = h.shape[1]
    start = pl.multiple_of(lax.axis_index("tp") * feats, feats)
    for w, out in ((wk, keys), (wv, values)):
        out[...] = dot(h[...], w[pl.ds(start, feats), :])


def begin(mine, w_key, w_value, ready):
    vmem = pl.BlockSpec(memory_space=pltpu.VMEM)
    return pl.pallas_call(
        begin_kernel,
        in_specs=[vmem] * 3 + [pl.BlockSpec(memory_space=pl.ANY)],
        out_specs=[vmem] * 2,
        out_shape=[jax.ShapeDtypeStruct((mine.shape[0], w.shape[1]), f32) for w in (w_key, w_value)],
        compiler_params=pltpu.CompilerParams(vmem_limit_bytes=6 * 2**20),
        cost_estimate=pl.CostEstimate(flops=0, bytes_accessed=48 * 2**20, transcendentals=0),
    )(mine, w_key, w_value, ready)


def project_kernel(h0, h1, h2, h3, k0, v0, wq, wk, wv, queries, keys, values):
    feats = h0.shape[1]
    totals = [0.0, k0[...], v0[...]]
    for s, h in enumerate((h0, h1, h2, h3)):
        start = pl.multiple_of(lax.rem(lax.axis_index("tp") + TP - s, TP) * feats, feats)
        rows = h[...]
        for m, w in enumerate((wq, wk, wv)):
            if s > 0 or m == 0:
                totals[m] = totals[m] + dot(rows, w[pl.ds(start, feats), :])
    q = totals[0].astype(bf16)
    for c in range(CTX):
        queries[c] = q
    keys[...] = totals[1].astype(bf16)
    values[...] = totals[2].astype(bf16)


def project(pieces, begun, w_query, w_key, w_value):
    rows, feats = pieces[0].shape
    vmem = pl.BlockSpec(memory_space=pltpu.VMEM)
    shapes = [(CTX, rows, w_query.shape[1]), (rows, w_key.shape[1]), (rows, w_value.shape[1])]
    return pl.pallas_call(
        project_kernel,
        in_specs=[vmem] * 9,
        out_specs=[vmem] * 3,
        out_shape=[jax.ShapeDtypeStruct(s, bf16) for s in shapes],
        compiler_params=pltpu.CompilerParams(vmem_limit_bytes=6 * 2**20),
    )(*pieces, *begun, w_query, w_key, w_value)


def split3(x):
    hi = x.astype(bf16).astype(f32)
    mid = (x - hi).astype(bf16).astype(f32)
    return hi, mid, x - hi - mid


def attend_kernel(len_ref, q, k, v, ks, vs, out, *, rows, chunk):
    scale = (HEAD ** -0.5) * math.log2(math.e)
    groups = 4
    keys = k.shape[1]
    share = ks.shape[0]
    starts = range(0, keys, chunk)
    units = [(r, kv) for r in range(0, q.shape[0], rows) for kv in range(2)]
    lane = lax.broadcasted_iota(jnp.int32, (rows, HEAD), 1)
    key_at = lax.broadcasted_iota(jnp.int32, (groups * rows, share), 1) + lax.axis_index("ctx") * share
    row_at = lax.rem(lax.broadcasted_iota(jnp.int32, (groups * rows, share), 0), rows)
    ones = jnp.ones((share, HEAD), bf16)
    chunk_at = lax.broadcasted_iota(jnp.int32, (chunk, HEAD), 0)
    counted = [jnp.where(chunk_at < len_ref[0] - c, 1.0, 0.0).astype(bf16) for c in starts]
    fill = [[(1 - count) * k[kv, 0:1, :] for count in counted] for kv in range(2)]

    def keys_of(kv, n):
        block = k[kv, n * chunk : (n + 1) * chunk, :]
        return block + fill[kv][n] if n else block

    def heads_of(r, kv):
        cols = [(kv * groups + g) * HEAD for g in range(groups)]
        return jnp.concatenate([q[r : r + rows, c : c + HEAD] for c in cols], 0)

    def of_kv(ref, kv):
        return ref[:, kv * HEAD : (kv + 1) * HEAD]

    heads = heads_of(*units[0])
    scores = [dot_nt(heads, keys_of(0, n)) for n in range(len(starts))]
    for n, (r, kv) in enumerate(units):
        self_scores = jnp.where(key_at <= row_at + r, dot_nt(heads, of_kv(ks, kv)), -1e30)
        tops = [s[:, c : c + HEAD] for s in scores for c in range(0, chunk, HEAD)]
        top = jnp.max(functools.reduce(jnp.maximum, tops), -1, keepdims=True)
        top = jnp.maximum(top, jnp.max(self_scores, -1, keepdims=True))
        weigh = lambda s: jnp.exp2((s - top) * scale).astype(bf16)
        acc = dot(weigh(self_scores), jnp.concatenate([of_kv(vs, kv), ones], 1))
        after = units[n + 1] if n + 1 < len(units) else None
        if after:
            heads = heads_of(*after)
        upcoming = []
        for m, (c, s, count) in enumerate(zip(starts, scores, counted)):
            if after:
                upcoming.append(dot_nt(heads, keys_of(after[1], m)))
            acc += dot(weigh(s), jnp.concatenate([v[kv, c : c + chunk, :], count], 1))
        scores = upcoming
        if kv == 0:
            tops_at = sums_at = jnp.zeros((rows, HEAD), f32)
        for g in range(groups):
            h = kv * groups + g
            part = acc[g * rows : (g + 1) * rows]
            out[r : r + rows, h * HEAD : (h + 1) * HEAD] = part[:, :HEAD].astype(bf16)
            tops_at = jnp.where(lane == h, top[g * rows : (g + 1) * rows], tops_at)
            sums_at = jnp.where(lane == h, part[:, HEAD:], sums_at)
        if kv == 1:
            fields = split3(tops_at) + split3(sums_at)
            side = fields[0] + sum(pltpu.roll(x, 8 * f, 1) for f, x in enumerate(fields) if f)
            out[r : r + rows, 8 * HEAD : 9 * HEAD] = side.astype(bf16)


def attend(length, q, k, v, ks, vs, rows=128, chunk=512):
    count, width = q.shape
    vmem = pl.BlockSpec(memory_space=pltpu.VMEM)
    smem = pl.BlockSpec(memory_space=pltpu.SMEM)
    return pl.pallas_call(
        functools.partial(attend_kernel, rows=rows, chunk=chunk),
        in_specs=[smem] + [vmem] * 5,
        out_specs=vmem,
        out_shape=jax.ShapeDtypeStruct((count, width + HEAD), bf16),
        compiler_params=pltpu.CompilerParams(vmem_limit_bytes=24 * 2**20),
        cost_estimate=pl.CostEstimate(flops=0, bytes_accessed=32 * 2**20, transcendentals=0),
    )(length, q, k, v, ks, vs)


def finish_kernel(parts, w, *outs, shifts):
    scale = (HEAD ** -0.5) * math.log2(math.e)
    side = [parts[p, :, 8 * HEAD : 9 * HEAD].astype(f32) for p in range(CTX)]
    tops = [s[:, 0:8] + s[:, 8:16] + s[:, 16:24] for s in side]
    sums = [s[:, 24:32] + s[:, 32:40] + s[:, 40:48] for s in side]
    top = functools.reduce(jnp.maximum, tops)
    scales = [jnp.exp2((m - top) * scale) for m in tops]
    total = sum(a * b for a, b in zip(scales, sums))
    block = outs[0].shape[1]
    starts = [pl.multiple_of(lax.rem(lax.axis_index("tp") + s, TP) * block, block) for s in shifts]
    sums_out = [0.0] * len(shifts)
    for first in range(0, 8, 2):
        heads = []
        for h in (first, first + 1):
            acc = sum(
                parts[p, :, h * HEAD : (h + 1) * HEAD].astype(f32) * scales[p][:, h : h + 1] for p in range(CTX)
            )
            heads.append((acc / total[:, h : h + 1]).astype(bf16))
        attended = jnp.concatenate(heads, 1)
        rows = pl.ds(first * HEAD, 2 * HEAD)
        sums_out = [o + dot(attended, w[rows, pl.ds(c, block)]) for o, c in zip(sums_out, starts)]
    for out, value in zip(outs, sums_out):
        out[...] = value.astype(bf16)


def finish(parts, w_out, shifts):
    share = parts.shape[1]
    block = w_out.shape[1] // TP
    vmem = pl.BlockSpec(memory_space=pltpu.VMEM)
    return pl.pallas_call(
        functools.partial(finish_kernel, shifts=shifts),
        in_specs=[vmem] * 2,
        out_specs=[vmem] * len(shifts),
        out_shape=[jax.ShapeDtypeStruct((share, block), bf16) for _ in shifts],
        compiler_params=pltpu.CompilerParams(vmem_limit_bytes=6 * 2**20),
        cost_estimate=pl.CostEstimate(
            flops=2 * share * w_out.size, bytes_accessed=2 * w_out.size, transcendentals=0
        ),
    )(parts, w_out)


def shift(x, s):
    return lax.ppermute(x, "tp", [(i, (i + s) % TP) for i in range(TP)])


def local(response, owner, doc_lengths, doc_keys, doc_values, w_query, w_key, w_value, w_out):
    count, feats = response.shape[1:]
    share = count // CTX
    cache = doc_keys.shape[0]
    chunks = lax.all_to_all(response[0].reshape(CTX, share, feats), "ctx", 0, 0)
    chunks, owner, doc_lengths, doc_keys, doc_values = lax.optimization_barrier(
        (chunks, owner, doc_lengths, doc_keys, doc_values)
    )
    mine = lax.dynamic_index_in_dim(chunks, owner[0], 0, keepdims=False)
    pieces = [mine] + [shift(mine, s) for s in range(1, TP)]
    visible = (jnp.arange(cache) < doc_lengths[0])[:, None, None]
    keys = jnp.where(visible, doc_keys, 0).transpose(1, 0, 2)
    values = jnp.where(visible, doc_values, 0).transpose(1, 0, 2)
    begun = begin(mine, w_key, w_value, keys)
    queries, self_keys, self_values = project(pieces, begun, w_query, w_key, w_value)
    queries, keys, values, self_keys, self_values, doc_lengths = lax.optimization_barrier(
        (queries, keys, values, self_keys, self_values, doc_lengths)
    )
    queries = lax.all_to_all(queries, "ctx", 0, 0).reshape(count, -1)
    sent = attend(doc_lengths, queries, keys, values, self_keys, self_values)
    parts = lax.all_to_all(sent.reshape(CTX, share, -1), "ctx", 0, 0)
    *away, own = finish(parts, w_out, (2, 1, 3, 0))
    away = [shift(x, s) for x, s in zip(away, (2, 1, 3))]
    return sum(x.astype(f32) for x in (own, *away)).astype(bf16)


def solution(mesh):
    placed = (
        P(("dp", "ctx"), None, "tp"),
        P("dp"),
        P(("dp", "ctx")),
        P(("dp", "ctx"), "tp", None),
        P(("dp", "ctx"), "tp", None),
        P(None, "tp"),
        P(None, "tp"),
        P(None, "tp"),
        P("tp", None),
    )
    return jax.shard_map(
        local, mesh=mesh, in_specs=placed, out_specs=P(("dp", "ctx"), "tp"), check_vma=False
    )
```

```python
import functools
import math

import jax
import jax.numpy as jnp
from jax import lax
from jax.experimental import pallas as pl
from jax.experimental.pallas import tpu as pltpu
from jax.sharding import PartitionSpec as P

CTX = 16
TP = 4
HEAD = 128
bf16 = jnp.bfloat16
f32 = jnp.float32


def dot(a, b):
    return jnp.dot(a, b, preferred_element_type=f32)


def dot_nt(a, b):
    return lax.dot_general(a, b, (((1,), (1,)), ((), ())), preferred_element_type=f32)


def begin_kernel(h, wk, wv, ready, keys, values):
    feats = h.shape[1]
    start = pl.multiple_of(lax.axis_index("tp") * feats, feats)
    for w, out in ((wk, keys), (wv, values)):
        out[...] = dot(h[...], w[pl.ds(start, feats), :])


def begin(mine, w_key, w_value, ready):
    vmem = pl.BlockSpec(memory_space=pltpu.VMEM)
    return pl.pallas_call(
        begin_kernel,
        in_specs=[vmem] * 3 + [pl.BlockSpec(memory_space=pl.ANY)],
        out_specs=[vmem] * 2,
        out_shape=[jax.ShapeDtypeStruct((mine.shape[0], w.shape[1]), f32) for w in (w_key, w_value)],
        compiler_params=pltpu.CompilerParams(vmem_limit_bytes=6 * 2**20),
        cost_estimate=pl.CostEstimate(flops=0, bytes_accessed=48 * 2**20, transcendentals=0),
    )(mine, w_key, w_value, ready)


def project_kernel(h0, h1, h2, h3, k0, v0, wq, wk, wv, queries, keys, values):
    feats = h0.shape[1]
    starts = [pl.multiple_of(lax.rem(lax.axis_index("tp") + TP - s, TP) * feats, feats) for s in range(TP)]
    pieces = [h[...] for h in (h0, h1, h2, h3)]
    q = sum(dot(h, wq[pl.ds(c, feats), :]) for h, c in zip(pieces, starts)).astype(bf16)
    for c in range(CTX):
        queries[c] = q
    for out, begun, w in ((keys, k0, wk), (values, v0, wv)):
        total = begun[...]
        for h, c in zip(pieces[1:], starts[1:]):
            total = total + dot(h, w[pl.ds(c, feats), :])
        out[...] = total.astype(bf16)


def project(pieces, begun, w_query, w_key, w_value):
    rows, feats = pieces[0].shape
    vmem = pl.BlockSpec(memory_space=pltpu.VMEM)
    shapes = [(CTX, rows, w_query.shape[1]), (rows, w_key.shape[1]), (rows, w_value.shape[1])]
    return pl.pallas_call(
        project_kernel,
        in_specs=[vmem] * 9,
        out_specs=[vmem] * 3,
        out_shape=[jax.ShapeDtypeStruct(s, bf16) for s in shapes],
        compiler_params=pltpu.CompilerParams(vmem_limit_bytes=6 * 2**20),
    )(*pieces, *begun, w_query, w_key, w_value)


def split3(x):
    hi = x.astype(bf16).astype(f32)
    mid = (x - hi).astype(bf16).astype(f32)
    return hi, mid, x - hi - mid


def attend_kernel(len_ref, q, k, v, ks, vs, out, *, rows, chunk):
    scale = (HEAD ** -0.5) * math.log2(math.e)
    groups = 4
    keys = k.shape[1]
    share = ks.shape[0]
    starts = range(0, keys, chunk)
    units = [(r, kv) for r in range(0, q.shape[0], rows) for kv in range(2)]
    lane = lax.broadcasted_iota(jnp.int32, (rows, HEAD), 1)
    key_at = lax.broadcasted_iota(jnp.int32, (groups * rows, share), 1) + lax.axis_index("ctx") * share
    row_at = lax.rem(lax.broadcasted_iota(jnp.int32, (groups * rows, share), 0), rows)
    ones = jnp.ones((share, HEAD), bf16)
    chunk_at = lax.broadcasted_iota(jnp.int32, (chunk, HEAD), 0)
    counted = [jnp.where(chunk_at < len_ref[0] - c, 1.0, 0.0).astype(bf16) for c in starts]
    fill = [[(1 - count) * k[kv, 0:1, :] for count in counted] for kv in range(2)]

    def keys_of(kv, n):
        block = k[kv, n * chunk : (n + 1) * chunk, :]
        return block + fill[kv][n] if n else block

    def heads_of(r, kv):
        cols = [(kv * groups + g) * HEAD for g in range(groups)]
        return jnp.concatenate([q[r : r + rows, c : c + HEAD] for c in cols], 0)

    def of_kv(ref, kv):
        return ref[:, kv * HEAD : (kv + 1) * HEAD]

    heads = heads_of(*units[0])
    scores = [dot_nt(heads, keys_of(0, n)) for n in range(len(starts))]
    for n, (r, kv) in enumerate(units):
        self_scores = jnp.where(key_at <= row_at + r, dot_nt(heads, of_kv(ks, kv)), -1e30)
        tops = [s[:, c : c + HEAD] for s in scores for c in range(0, chunk, HEAD)]
        top = jnp.max(functools.reduce(jnp.maximum, tops), -1, keepdims=True)
        top = jnp.maximum(top, jnp.max(self_scores, -1, keepdims=True))
        weigh = lambda s: jnp.exp2((s - top) * scale).astype(bf16)
        acc = dot(weigh(self_scores), jnp.concatenate([of_kv(vs, kv), ones], 1))
        after = units[n + 1] if n + 1 < len(units) else None
        if after:
            heads = heads_of(*after)
        upcoming = []
        for m, (c, s, count) in enumerate(zip(starts, scores, counted)):
            if after:
                upcoming.append(dot_nt(heads, keys_of(after[1], m)))
            acc += dot(weigh(s), jnp.concatenate([v[kv, c : c + chunk, :], count], 1))
        scores = upcoming
        if kv == 0:
            tops_at = sums_at = jnp.zeros((rows, HEAD), f32)
        for g in range(groups):
            h = kv * groups + g
            part = acc[g * rows : (g + 1) * rows]
            out[r : r + rows, h * HEAD : (h + 1) * HEAD] = part[:, :HEAD].astype(bf16)
            tops_at = jnp.where(lane == h, top[g * rows : (g + 1) * rows], tops_at)
            sums_at = jnp.where(lane == h, part[:, HEAD:], sums_at)
        if kv == 1:
            fields = split3(tops_at) + split3(sums_at)
            side = fields[0] + sum(pltpu.roll(x, 8 * f, 1) for f, x in enumerate(fields) if f)
            out[r : r + rows, 8 * HEAD : 9 * HEAD] = side.astype(bf16)


def attend(length, q, k, v, ks, vs, rows=128, chunk=512):
    count, width = q.shape
    vmem = pl.BlockSpec(memory_space=pltpu.VMEM)
    smem = pl.BlockSpec(memory_space=pltpu.SMEM)
    return pl.pallas_call(
        functools.partial(attend_kernel, rows=rows, chunk=chunk),
        in_specs=[smem] + [vmem] * 5,
        out_specs=vmem,
        out_shape=jax.ShapeDtypeStruct((count, width + HEAD), bf16),
        compiler_params=pltpu.CompilerParams(vmem_limit_bytes=24 * 2**20),
        cost_estimate=pl.CostEstimate(flops=0, bytes_accessed=32 * 2**20, transcendentals=0),
    )(length, q, k, v, ks, vs)


def finish_kernel(parts, w, *outs, shifts):
    scale = (HEAD ** -0.5) * math.log2(math.e)
    side = [parts[p, :, 8 * HEAD : 9 * HEAD].astype(f32) for p in range(CTX)]
    tops = [s[:, 0:8] + s[:, 8:16] + s[:, 16:24] for s in side]
    sums = [s[:, 24:32] + s[:, 32:40] + s[:, 40:48] for s in side]
    top = functools.reduce(jnp.maximum, tops)
    scales = [jnp.exp2((m - top) * scale) for m in tops]
    total = sum(a * b for a, b in zip(scales, sums))
    block = outs[0].shape[1]
    starts = [pl.multiple_of(lax.rem(lax.axis_index("tp") + s, TP) * block, block) for s in shifts]
    sums_out = [0.0] * len(shifts)
    for first in range(0, 8, 2):
        heads = []
        for h in (first, first + 1):
            acc = sum(
                parts[p, :, h * HEAD : (h + 1) * HEAD].astype(f32) * scales[p][:, h : h + 1] for p in range(CTX)
            )
            heads.append((acc / total[:, h : h + 1]).astype(bf16))
        attended = jnp.concatenate(heads, 1)
        rows = pl.ds(first * HEAD, 2 * HEAD)
        sums_out = [o + dot(attended, w[rows, pl.ds(c, block)]) for o, c in zip(sums_out, starts)]
    for out, value in zip(outs, sums_out):
        out[...] = value.astype(bf16)


def finish(parts, w_out, shifts):
    share = parts.shape[1]
    block = w_out.shape[1] // TP
    vmem = pl.BlockSpec(memory_space=pltpu.VMEM)
    return pl.pallas_call(
        functools.partial(finish_kernel, shifts=shifts),
        in_specs=[vmem] * 2,
        out_specs=[vmem] * len(shifts),
        out_shape=[jax.ShapeDtypeStruct((share, block), bf16) for _ in shifts],
        compiler_params=pltpu.CompilerParams(vmem_limit_bytes=6 * 2**20),
        cost_estimate=pl.CostEstimate(
            flops=2 * share * w_out.size, bytes_accessed=2 * w_out.size, transcendentals=0
        ),
    )(parts, w_out)


def shift(x, s):
    return lax.ppermute(x, "tp", [(i, (i + s) % TP) for i in range(TP)])


def local(response, owner, doc_lengths, doc_keys, doc_values, w_query, w_key, w_value, w_out):
    count, feats = response.shape[1:]
    share = count // CTX
    cache = doc_keys.shape[0]
    chunks = lax.all_to_all(response[0].reshape(CTX, share, feats), "ctx", 0, 0)
    chunks, owner, doc_lengths, doc_keys, doc_values = lax.optimization_barrier(
        (chunks, owner, doc_lengths, doc_keys, doc_values)
    )
    mine = lax.dynamic_index_in_dim(chunks, owner[0], 0, keepdims=False)
    pieces = [mine] + [shift(mine, s) for s in range(1, TP)]
    visible = (jnp.arange(cache) < doc_lengths[0])[:, None, None]
    keys = jnp.where(visible, doc_keys, 0).transpose(1, 0, 2)
    values = jnp.where(visible, doc_values, 0).transpose(1, 0, 2)
    begun = begin(mine, w_key, w_value, keys)
    queries, self_keys, self_values = project(pieces, begun, w_query, w_key, w_value)
    queries, keys, values, self_keys, self_values, doc_lengths = lax.optimization_barrier(
        (queries, keys, values, self_keys, self_values, doc_lengths)
    )
    queries = lax.all_to_all(queries, "ctx", 0, 0).reshape(count, -1)
    sent = attend(doc_lengths, queries, keys, values, self_keys, self_values)
    parts = lax.all_to_all(sent.reshape(CTX, share, -1), "ctx", 0, 0)
    *away, own = finish(parts, w_out, (2, 1, 3, 0))
    away = [shift(x, s) for x, s in zip(away, (2, 1, 3))]
    return sum(x.astype(f32) for x in (own, *away)).astype(bf16)


def solution(mesh):
    placed = (
        P(("dp", "ctx"), None, "tp"),
        P("dp"),
        P(("dp", "ctx")),
        P(("dp", "ctx"), "tp", None),
        P(("dp", "ctx"), "tp", None),
        P(None, "tp"),
        P(None, "tp"),
        P(None, "tp"),
        P("tp", None),
    )
    return jax.shard_map(
        local, mesh=mesh, in_specs=placed, out_specs=P(("dp", "ctx"), "tp"), check_vma=False
    )
```
